32 devices in a mesh: role: 2 (over x), shard: 4 (over z), rep: 4 (over y, core).
Axes of the slice: x: 2, y: 2, z: 4, core: 2. Of those that a mesh axis runs over, the one named last changes fastest.
Arguments:
- qkv_versions: bfloat16 [2, 5120, 7168], P('role', 'rep', 'shard'), may hold values from -0.078125 to 0.078125
- qkv_bias: bfloat16 [2, 7168], P('role'), may hold values from -3 to 3
- o_versions: bfloat16 [2, 5120, 5120], P('role', 'rep', 'shard'), may hold values from -0.078125 to 0.078125
- norm_gain: bfloat16 [2, 5120], P('role'), may hold values from 0.5 to 1.5
- hidden: bfloat16 [2, 256, 4, 5120], P('role', ('shard', 'rep')), may hold values from -6 to 6
- cache_keys: bfloat16 [2, 256, 128, 1024], P('role', ('shard', 'rep')), may hold values from -220 to 220
- cache_values: bfloat16 [2, 256, 128, 1024], P('role', ('shard', 'rep')), may hold values from -6 to 6
- lengths: int32 [2, 256], P('role', ('shard', 'rep')), may hold values from 2 to 128, as said below
Outputs:
- layer_out: bfloat16 [2, 256, 4, 5120], P('role', ('shard', 'rep'))
- new_qkv: bfloat16 [2, 5120, 7168], P('role', 'rep', 'shard')
- new_o: bfloat16 [2, 5120, 5120], P('role', 'rep', 'shard')
The draws below stay inside these ranges and needn't reach their ends.
Inputs may be any that keep to these rules, and one draw needn't show every extreme that they name: `lengths`: in every aligned group of 16 rows of a role at least one row has all 128 positions live.
All inputs are finite; a program needn't handle non-finite values.
Results may differ from the reference program's by a relative error of at most 0.0065.
The reference program's roundings to bfloat16 on the way count: a program that leaves them out, or rounds other values in their place, can miss the bound.
Values may be sent and summed in bfloat16 or wider, within the bound.
A program may use at most 128 MiB of HBM per device.

```python
import math
import jax
import jax.numpy as jnp
from jax import lax

FACTOR_A = 40
FACTOR_B = 128
D = 5120
HEADS = 40
KV_HEADS = 8
HEAD_DIM = 128
QDIM = 5120
KVD = 1024
QKV = 7168
ROWS_DEV = 16
CACHE = 128
STEPS = 4
ROWS = 256
N_ROLE = 2


def draw_cache_keys(key, part):
    shape = (N_ROLE, ROWS, CACHE, KVD)
    scaled = jnp.clip(2.0 * jax.random.normal(key, shape, jnp.float32), -12.0, 12.0)
    return scaled.astype(jnp.bfloat16)


def draw_lengths(key, part):
    base = jax.random.randint(key, (N_ROLE, ROWS), 2, CACHE + 1, dtype=jnp.int32)
    groups = ROWS // ROWS_DEV
    chosen = jax.random.randint(jax.random.fold_in(key, 7), (N_ROLE, groups, 1), 0, ROWS_DEV, dtype=jnp.int32)
    within = jnp.arange(ROWS_DEV, dtype=jnp.int32).reshape(1, 1, ROWS_DEV)
    filled = (within == chosen).reshape(N_ROLE, ROWS)
    return jnp.where(filled, CACHE, base).astype(jnp.int32)


def levels(own_key, extent, cuts, low, largest):
    def one(dim, blocks):
        draws = jax.random.uniform(jax.random.fold_in(jax.random.fold_in(own_key, 6), dim), (blocks,), jnp.float32, low / len(cuts), largest / len(cuts))
        return jnp.repeat(jnp.exp(draws), extent[dim] // blocks).reshape((-1,) + (1,) * (len(extent) - dim - 1))

    loudness = one(*cuts[0])
    for cut in cuts[1:]:
        loudness = loudness * one(*cut)
    return loudness


def noise(key, dims, scale, limit, split=(), kind=jnp.bfloat16):
    entries = jax.random.normal(key, dims, jnp.float32) * scale
    if len(split) > 0:
        entries = levels(key, dims, split, -0.22, 0.18) * entries
    return jnp.clip(entries, min=-limit, max=limit).astype(kind)


def setup_inputs(seed: int = 0) -> dict:
    key_of = jax.random.split(jax.random.key(seed), 9)
    return {
        "qkv_versions": noise(key_of[0], (N_ROLE, D, QKV), D ** -0.5, 0.078125, ((0, 2), (1, 4), (2, 4))),
        "qkv_bias": noise(key_of[1], (N_ROLE, QKV), 0.5, 3.0, ((0, 2),)),
        "o_versions": noise(key_of[2], (N_ROLE, QDIM, D), QDIM ** -0.5, 0.078125, ((0, 2), (1, 4), (2, 4))),
        "norm_gain": jnp.clip(1.0 + 0.1 * jax.random.normal(key_of[3], (N_ROLE, D), jnp.float32), 0.5, 1.5).astype(jnp.bfloat16),
        "hidden": noise(key_of[4], (N_ROLE, ROWS, STEPS, D), 1.0, 6.0, ((0, 2), (1, 16))),
        "cache_keys": draw_cache_keys(jax.random.fold_in(key_of[8], 71), 0),
        "cache_values": noise(key_of[6], (N_ROLE, ROWS, CACHE, KVD), 1.0, 6.0, ((0, 2), (1, 16))),
        "lengths": draw_lengths(jax.random.fold_in(key_of[8], 71), 0),
    }


EPSILON = 1e-06
ROPE_BASE = 1000000.0

def hadamard_pair():
    modulus = FACTOR_A // 2 - 1
    residues = jnp.arange(modulus, dtype=jnp.int32)
    squares = jnp.arange(1, modulus, dtype=jnp.int32) ** 2 % modulus
    differ = (residues[None, :] - residues[:, None]) % modulus
    residue_mask = jnp.any(differ[:, :, None] == squares[None, None, :], axis=2)
    jacobs = jnp.where(differ == 0, 0.0, jnp.where(residue_mask, 1.0, -1.0)).astype(jnp.float32)
    top_row = jnp.concatenate([jnp.zeros((1, 1), jnp.float32), jnp.ones((1, modulus), jnp.float32)], axis=1)
    lower_rows = jnp.concatenate([-jnp.ones((modulus, 1), jnp.float32), jacobs], axis=1)
    paley_core = jnp.eye(modulus + 1, dtype=jnp.float32) + jnp.concatenate([top_row, lower_rows], axis=0)
    doubler = jnp.array([[1.0, 1.0], [1.0, -1.0]], jnp.float32)
    outer_factor = jnp.kron(doubler, paley_core)
    indices = jnp.arange(FACTOR_B, dtype=jnp.int32)
    common_bits = indices[:, None] & indices[None, :]
    parity = jnp.zeros((FACTOR_B, FACTOR_B), jnp.int32)
    for bit_level in range(FACTOR_B.bit_length() - 1):
        parity = parity + (common_bits >> bit_level & 1)
    inner_factor = (1 - 2 * (parity % 2)).astype(jnp.float32)
    return (outer_factor, inner_factor)

def rotate_rows(matrix):
    outer_factor, inner_factor = hadamard_pair()
    blocks = matrix.reshape(FACTOR_A, FACTOR_B, -1)
    turned = jnp.einsum('abc,ax,by->xyc', blocks, outer_factor, inner_factor, precision=lax.Precision.HIGHEST)
    return turned.reshape(D, -1) / math.sqrt(D)

def rotary(vectors, positions):
    half_dim = HEAD_DIM // 2
    frequency = jnp.power(jnp.float32(ROPE_BASE), -jnp.arange(0, HEAD_DIM, 2, dtype=jnp.float32) / HEAD_DIM)
    angles = positions.astype(jnp.float32)[:, :, None] * frequency[None, None, :]
    cosine = jnp.cos(angles)[:, :, None, :]
    sine = jnp.sin(angles)[:, :, None, :]
    first, second = (vectors[..., :half_dim], vectors[..., half_dim:])
    return jnp.concatenate([first * cosine - second * sine, second * cosine + first * sine], axis=-1)

def normalize(states, gain):
    mean_square = lax.optimization_barrier(jnp.mean(states * states, axis=-1, keepdims=True))
    return (states * lax.rsqrt(mean_square + EPSILON) * gain.astype(jnp.float32)).astype(jnp.bfloat16)

def attend(packed, keys, values, lengths):
    rows = packed.shape[0]
    group_size = HEADS // KV_HEADS
    positions = lengths[:, None] + jnp.arange(STEPS, dtype=jnp.int32)[None, :]
    queries = rotary(packed[:, :, :QDIM].astype(jnp.float32).reshape(rows, STEPS, HEADS, HEAD_DIM), positions).astype(jnp.bfloat16)
    new_keys = rotary(packed[:, :, QDIM:QDIM + KVD].astype(jnp.float32).reshape(rows, STEPS, KV_HEADS, HEAD_DIM), positions).astype(jnp.bfloat16)
    new_values = packed[:, :, QDIM + KVD:].reshape(rows, STEPS, KV_HEADS, HEAD_DIM)
    queries = queries.reshape(rows, STEPS, KV_HEADS, group_size, HEAD_DIM).astype(jnp.float32)
    cached_keys = keys.reshape(rows, CACHE, KV_HEADS, HEAD_DIM).astype(jnp.float32)
    cached_values = values.reshape(rows, CACHE, KV_HEADS, HEAD_DIM).astype(jnp.float32)
    score_scale = 1.0 / math.sqrt(HEAD_DIM)
    old_scores = jnp.einsum('rtkgd,rpkd->rtkgp', queries, cached_keys) * score_scale
    fresh_scores = jnp.einsum('rtkgd,rskd->rtkgs', queries, new_keys.astype(jnp.float32)) * score_scale
    live_mask = jnp.arange(CACHE, dtype=jnp.int32)[None, :] < lengths[:, None]
    old_scores = jnp.where(live_mask[:, None, None, None, :], old_scores, -1e+30)
    causal = jnp.arange(STEPS, dtype=jnp.int32)[None, :] <= jnp.arange(STEPS, dtype=jnp.int32)[:, None]
    fresh_scores = jnp.where(causal[None, :, None, None, :], fresh_scores, -1e+30)
    row_peak = jnp.maximum(lax.optimization_barrier(jnp.max(old_scores, axis=-1, keepdims=True)), lax.optimization_barrier(jnp.max(fresh_scores, axis=-1, keepdims=True)))
    old_exp = jnp.exp(old_scores - row_peak)
    fresh_exp = jnp.exp(fresh_scores - row_peak)
    denominator = lax.optimization_barrier(jnp.sum(old_exp, axis=-1, keepdims=True)) + lax.optimization_barrier(jnp.sum(fresh_exp, axis=-1, keepdims=True))
    old_weights = (old_exp / denominator).astype(jnp.bfloat16).astype(jnp.float32)
    fresh_weights = (fresh_exp / denominator).astype(jnp.bfloat16).astype(jnp.float32)
    combined = jnp.einsum('rtkgp,rpkd->rtkgd', old_weights, cached_values)
    combined = combined + jnp.einsum('rtkgs,rskd->rtkgd', fresh_weights, new_values.astype(jnp.float32))
    return combined.reshape(rows, STEPS, QDIM).astype(jnp.bfloat16)

def layer_forward(qkv_weight, bias, out_weight, gain, hidden, keys, values, lengths):
    states = hidden.astype(jnp.float32)
    normed = normalize(states, gain)
    flat_rows = normed.reshape(-1, D)
    packed = jnp.dot(flat_rows, qkv_weight, preferred_element_type=jnp.float32) + bias.astype(jnp.float32)
    packed = packed.astype(jnp.bfloat16).reshape(ROWS, STEPS, QKV)
    blocks = ROWS // ROWS_DEV

    def one_block(items):
        return attend(items[0], items[1], items[2], items[3])
    attended = lax.map(one_block, (packed.reshape(blocks, ROWS_DEV, STEPS, QKV), keys.reshape(blocks, ROWS_DEV, CACHE, KVD), values.reshape(blocks, ROWS_DEV, CACHE, KVD), lengths.reshape(blocks, ROWS_DEV)))
    attended = attended.reshape(ROWS * STEPS, QDIM)
    projected = jnp.dot(attended, out_weight, preferred_element_type=jnp.float32).reshape(ROWS, STEPS, D)
    return (states + projected).astype(jnp.bfloat16)

def reference(qkv_versions, qkv_bias, o_versions, norm_gain, hidden, cache_keys, cache_values, lengths):
    outputs = []
    for role_slot in range(N_ROLE):
        outputs.append(layer_forward(qkv_versions[role_slot], qkv_bias[role_slot], o_versions[role_slot], norm_gain[role_slot], hidden[role_slot], cache_keys[role_slot], cache_values[role_slot], lengths[role_slot]))
    layer_out = jnp.stack(outputs)
    rotated_qkv = rotate_rows(qkv_versions[0].astype(jnp.float32)).astype(jnp.bfloat16)
    rotated_o = rotate_rows(o_versions[0].astype(jnp.float32).T).T.astype(jnp.bfloat16)
    new_qkv = jnp.stack([rotated_qkv] * N_ROLE)
    new_o = jnp.stack([rotated_o] * N_ROLE)
    return (layer_out, new_qkv, new_o)
```

```python
import functools
import math

import jax
import jax.numpy as jnp
import numpy as np
from jax import lax
from jax.experimental import pallas as pl
from jax.experimental.pallas import tpu as pltpu
from jax.sharding import PartitionSpec as P

FACTOR_A = 40
FACTOR_B = 128
D = 5120
HEADS = 40
KV_HEADS = 8
HEAD_DIM = 128
QDIM = 5120
KVD = 1024
STEPS = 4


EPSILON = 1e-06
ROPE_BASE = 1000000.0


MESH = pl.DeviceIdType.MESH


def rotation_core():
    modulus = FACTOR_A // 2 - 1
    squares = {k * k % modulus for k in range(1, modulus)}
    paley = np.ones((modulus + 1, modulus + 1), np.float32)
    paley[1:, 0] = -1.0
    for i in range(modulus):
        for j in range(modulus):
            if i != j:
                paley[i + 1, j + 1] = 1.0 if (j - i) % modulus in squares else -1.0
    inner = np.ones((1, 1), np.float32)
    while inner.shape[0] < FACTOR_B:
        inner = np.kron(inner, np.array([[1, 1], [1, -1]], np.float32))
    return np.kron(paley, inner).astype(jnp.bfloat16)


def exchange_kernel(shards, reps, chunks, normed, own_q, own_o, n_all, q_all, rec_o, w_o,
                    n_send, n_recv, y_send, y_recv, s_send, s_recv, f_send, f_recv,
                    x_send, x_recv, a_send, a_recv, load, store, q_hold, n_hold, o_hold):
    role, shard, rep = lax.axis_index("role"), lax.axis_index("shard"), lax.axis_index("rep")
    planes = reps // 2
    near = rep + 1 - 2 * lax.rem(rep, 2)
    far = [lax.rem(rep + 2 * h, reps) for h in range(planes)]
    back = [lax.rem(rep - 2 * h + reps, reps) for h in range(planes)]
    peer = [lax.rem(shard + k, shards) for k in range(shards)]

    greeted = [{"role": 1 - role}, {"rep": near}]
    greeted += [{"rep": far[h]} for h in range(1, planes)]
    greeted += [{"shard": peer[k]} for k in range(1, shards)]
    barrier = pltpu.get_barrier_semaphore()
    for device in greeted:
        pl.semaphore_signal(barrier, inc=1, device_id=device, device_id_type=MESH)
    pl.semaphore_wait(barrier, len(greeted))

    def remote(src, dst, send, recv, device):
        return pltpu.make_async_remote_copy(
            src_ref=src, dst_ref=dst, send_sem=send, recv_sem=recv,
            device_id=device, device_id_type=MESH)

    raw = remote(own_o.at[1], rec_o, x_send, x_recv, {"role": 1 - role})

    @pl.when(role == 0)
    def _():
        raw.start()

    tokens = [remote(normed, n_all.at[shard], n_send.at[k], n_recv.at[k], {"shard": peer[k]})
              for k in range(1, shards)]
    across = [[remote(own_q.at[c], q_all.at[rep, c], y_send.at[h - 1, c], y_recv.at[h - 1, c],
                      {"rep": far[h]}) for c in range(chunks)] for h in range(1, planes)]
    aside = remote(own_q, q_all.at[rep], s_send, s_recv, {"rep": near})
    onward = [[remote(q_all.at[back[h], c], q_all.at[back[h], c], f_send.at[h - 1, c],
                      f_recv.at[h - 1, c], {"rep": near}) for c in range(chunks)]
              for h in range(1, planes)]
    for c in range(chunks):
        for h in range(planes - 1):
            across[h][c].start()
    for copy in tokens:
        copy.start()
    aside.start()
    own_in = [pltpu.make_async_copy(own_q.at[c], q_hold.at[c], load.at[c]) for c in range(chunks)]
    own_in.append(pltpu.make_async_copy(normed, n_hold, load.at[chunks]))
    own_out = [pltpu.make_async_copy(q_hold.at[c], q_all.at[rep, c], store.at[c])
               for c in range(chunks)]
    own_out.append(pltpu.make_async_copy(n_hold, n_all.at[shard], store.at[chunks]))
    for copy in own_in:
        copy.start()

    def fold(source):
        copies = [remote(source.at[peer[k]], w_o.at[shard], a_send.at[k], a_recv.at[k],
                         {"shard": peer[k]}) for k in range(1, shards)]
        return (copies, pltpu.make_async_copy(source.at[shard], o_hold, load.at[chunks + 1]),
                pltpu.make_async_copy(o_hold, w_o.at[shard], store.at[chunks + 1]))

    @pl.when(role == 0)
    def _():
        copies, fetch, keep = fold(own_o.at[0])
        for copy in copies:
            copy.start()
        fetch.start()
        fetch.wait()
        keep.start()

    for fetched, stored in zip(own_in, own_out):
        fetched.wait()
        stored.start()

    for c in range(chunks):
        for h in range(planes - 1):
            across[h][c].wait_recv()
            onward[h][c].start()
        if c == min(1, chunks - 1):
            @pl.when(role == 1)
            def _():
                raw.wait_recv()
                copies, fetch, keep = fold(rec_o)
                for copy in copies:
                    copy.start()
                fetch.start()
                fetch.wait()
                keep.start()

    for copy in tokens:
        copy.wait()
    aside.wait()
    for copy in own_out:
        copy.wait()
    copies, _, keep = fold(rec_o)
    for copy in copies:
        copy.wait()
    keep.wait()
    for c in range(chunks):
        for h in range(planes - 1):
            across[h][c].wait_send()
            onward[h][c].wait()

    @pl.when(role == 0)
    def _():
        raw.wait_send()


def exchange(normed, own_q, own_o):
    shards, reps = lax.axis_size("shard"), lax.axis_size("rep")
    rows, width = normed.shape
    depth, columns = own_q.shape
    height, out_columns = own_o.shape
    chunks = 5 if depth % 80 == 0 else 1
    half = height // 2
    part = half // shards
    kind = normed.dtype
    dma = pltpu.SemaphoreType.DMA
    planes = max(reps // 2 - 1, 1)
    n_all, q_all, _, w_o = pl.pallas_call(
        functools.partial(exchange_kernel, shards, reps, chunks),
        out_shape=(
            jax.ShapeDtypeStruct((shards, rows, width), kind),
            jax.ShapeDtypeStruct((reps, chunks, depth // chunks, columns), kind),
            jax.ShapeDtypeStruct((shards, part, out_columns), kind),
            jax.ShapeDtypeStruct((shards, part, out_columns), kind),
        ),
        in_specs=[pl.BlockSpec(memory_space=pl.ANY)] * 3,
        out_specs=(pl.BlockSpec(memory_space=pl.ANY),) * 4,
        scratch_shapes=[
            dma((shards,)), dma((shards,)),
            dma((planes, chunks)), dma((planes, chunks)),
            dma, dma,
            dma((planes, chunks)), dma((planes, chunks)),
            dma, dma,
            dma((shards,)), dma((shards,)),
            dma((chunks + 2,)), dma((chunks + 2,)),
            pltpu.VMEM((chunks, depth // chunks, columns), kind),
            pltpu.VMEM((rows, width), kind),
            pltpu.VMEM((part, out_columns), kind),
        ],
        compiler_params=pltpu.CompilerParams(
            collective_id=0, has_side_effects=True, vmem_limit_bytes=16 * 1024 * 1024),
        name="exchange",
    )(normed, own_q.reshape(chunks, depth // chunks, columns),
      own_o.reshape(2, shards, part, out_columns))
    return n_all, q_all.reshape(reps * depth, columns), w_o


def rotate_row_part(full_rows, core, part_index, part_total):
    order = core.shape[0]
    per_half = part_total // 2
    sign = jnp.where(part_index < per_half, 1.0, -1.0).astype(jnp.float32)
    top = full_rows[:order].astype(jnp.float32)
    bottom = full_rows[order:].astype(jnp.float32)
    mixed = (top + sign * bottom).astype(jnp.bfloat16)
    count = order // per_half
    part = lax.dynamic_slice_in_dim(core, lax.rem(part_index, per_half) * count, count, 0)
    turned = jnp.dot(part, mixed, preferred_element_type=jnp.float32)
    return (turned * (1.0 / math.sqrt(D))).astype(jnp.bfloat16)


def rotate_columns(matrix, core):
    height = matrix.shape[0]
    order = core.shape[0]
    left = matrix[:, :order].astype(jnp.float32)
    right = matrix[:, order:].astype(jnp.float32)
    mixed = jnp.concatenate([left + right, left - right], axis=0).astype(jnp.bfloat16)
    turned = jnp.dot(mixed, core, preferred_element_type=jnp.float32)
    turned = (turned * (1.0 / math.sqrt(D))).astype(jnp.bfloat16)
    return jnp.concatenate([turned[:height], turned[height:]], axis=1)


def rotary(vectors, positions):
    half_dim = HEAD_DIM // 2
    frequency = jnp.power(
        jnp.float32(ROPE_BASE), -jnp.arange(0, HEAD_DIM, 2, dtype=jnp.float32) / HEAD_DIM
    )
    angles = positions.astype(jnp.float32)[:, :, None] * frequency[None, None, :]
    cosine = jnp.cos(angles)[:, :, None, :]
    sine = jnp.sin(angles)[:, :, None, :]
    first, second = (vectors[..., :half_dim], vectors[..., half_dim:])
    return jnp.concatenate(
        [first * cosine - second * sine, second * cosine + first * sine], axis=-1
    )


def normalize(states, gain):
    mean_square = jnp.mean(states * states, axis=-1, keepdims=True)
    return (states * lax.rsqrt(mean_square + EPSILON) * gain.astype(jnp.float32)).astype(
        jnp.bfloat16
    )


def attend(packed, keys, values, lengths):
    rows = packed.shape[0]
    cached = keys.shape[1]
    group_size = HEADS // KV_HEADS
    positions = lengths[:, None] + jnp.arange(STEPS, dtype=jnp.int32)[None, :]
    queries = rotary(
        packed[:, :, :QDIM].astype(jnp.float32).reshape(rows, STEPS, HEADS, HEAD_DIM), positions
    ).astype(jnp.bfloat16)
    new_keys = rotary(
        packed[:, :, QDIM : QDIM + KVD]
        .astype(jnp.float32)
        .reshape(rows, STEPS, KV_HEADS, HEAD_DIM),
        positions,
    ).astype(jnp.bfloat16)
    new_values = packed[:, :, QDIM + KVD :].reshape(rows, STEPS, KV_HEADS, HEAD_DIM)
    queries = queries.reshape(rows, STEPS, KV_HEADS, group_size, HEAD_DIM)
    cached_keys = keys.reshape(rows, cached, KV_HEADS, HEAD_DIM)
    cached_values = values.reshape(rows, cached, KV_HEADS, HEAD_DIM)
    score_scale = 1.0 / math.sqrt(HEAD_DIM)
    old_scores = (
        jnp.einsum("rtkgd,rpkd->rtkgp", queries, cached_keys, preferred_element_type=jnp.float32)
        * score_scale
    )
    fresh_scores = (
        jnp.einsum("rtkgd,rskd->rtkgs", queries, new_keys, preferred_element_type=jnp.float32)
        * score_scale
    )
    live_mask = jnp.arange(cached, dtype=jnp.int32)[None, :] < lengths[:, None]
    old_scores = jnp.where(live_mask[:, None, None, None, :], old_scores, -1e30)
    causal = (
        jnp.arange(STEPS, dtype=jnp.int32)[None, :] <= jnp.arange(STEPS, dtype=jnp.int32)[:, None]
    )
    fresh_scores = jnp.where(causal[None, :, None, None, :], fresh_scores, -1e30)
    row_peak = jnp.maximum(
        jnp.max(old_scores, axis=-1, keepdims=True), jnp.max(fresh_scores, axis=-1, keepdims=True)
    )
    old_exp = jnp.exp(old_scores - row_peak)
    fresh_exp = jnp.exp(fresh_scores - row_peak)
    denominator = jnp.sum(old_exp, axis=-1, keepdims=True) + jnp.sum(
        fresh_exp, axis=-1, keepdims=True
    )
    old_weights = (old_exp / denominator).astype(jnp.bfloat16)
    fresh_weights = (fresh_exp / denominator).astype(jnp.bfloat16)
    combined = jnp.einsum(
        "rtkgp,rpkd->rtkgd", old_weights, cached_values, preferred_element_type=jnp.float32
    )
    combined = combined + jnp.einsum(
        "rtkgs,rskd->rtkgd", fresh_weights, new_values, preferred_element_type=jnp.float32
    )
    return combined.reshape(rows, STEPS, QDIM).astype(jnp.bfloat16)


def body(qkv_versions, qkv_bias, o_versions, norm_gain, hidden, cache_keys, cache_values, lengths):
    trainer_side = lax.axis_index("role") == 0
    shard_index = lax.axis_index("shard")
    rep_index = lax.axis_index("rep")
    rep_total = lax.axis_size("rep")
    own_qkv = qkv_versions[0]
    own_out = o_versions[0]
    states = hidden[0].astype(jnp.float32)
    normed = normalize(states, norm_gain[0])
    piece, full_qkv, folded = exchange(normed.reshape(-1, D), own_qkv, own_out)
    late_out, _ = lax.optimization_barrier((own_out, piece))
    full_out = lax.all_gather(late_out, "rep", axis=0, tiled=True)
    core = jnp.asarray(rotation_core())

    column_count = full_qkv.shape[1]
    bias_columns = lax.dynamic_slice_in_dim(
        qkv_bias[0], shard_index * column_count, column_count
    ).astype(jnp.float32)
    product = jnp.dot(piece.reshape(-1, D), full_qkv, preferred_element_type=jnp.float32)
    packed_columns = (product.reshape(-1, STEPS, column_count) + bias_columns).astype(
        jnp.bfloat16
    )
    turned_out = rotate_columns(jnp.swapaxes(folded, 0, 1).reshape(folded.shape[1], D), core)
    turned_qkv = rotate_row_part(full_qkv, core.T, rep_index, rep_total)
    packed = lax.all_to_all(packed_columns, "shard", split_axis=0, concat_axis=2, tiled=True)
    mine = lax.all_to_all(turned_out, "shard", split_axis=1, concat_axis=0, tiled=True)
    sent_qkv = lax.ppermute(turned_qkv, "role", [(0, 1)])

    packed, turned_qkv, _ = lax.optimization_barrier((packed, turned_qkv, turned_out))
    attended = attend(packed, cache_keys[0], cache_values[0], lengths[0])
    attended, full_out, mine = lax.optimization_barrier((attended, full_out, mine))
    theirs = lax.ppermute(mine, "role", [(0, 1), (1, 0)])
    out_width = full_out.shape[1]
    piece = lax.all_gather(attended, "shard", axis=0, tiled=True)
    product = jnp.dot(piece.reshape(-1, QDIM), full_out, preferred_element_type=jnp.float32)
    projected_columns = product.reshape(piece.shape[0], STEPS, out_width).astype(jnp.bfloat16)
    projected = lax.all_to_all(projected_columns, "shard", split_axis=0, concat_axis=2, tiled=True)
    layer_out = (states + projected.astype(jnp.float32)).astype(jnp.bfloat16)[None]

    new_qkv = jnp.where(trainer_side, turned_qkv, sent_qkv)
    new_o = jnp.concatenate(
        [jnp.where(trainer_side, mine, theirs), jnp.where(trainer_side, theirs, mine)], axis=0
    )
    return (layer_out, new_qkv[None], new_o[None])


def solution(mesh):
    in_specs = (
        P("role", "rep", "shard"),
        P("role", None),
        P("role", "rep", "shard"),
        P("role", None),
        P("role", ("shard", "rep"), None, None),
        P("role", ("shard", "rep"), None, None),
        P("role", ("shard", "rep"), None, None),
        P("role", ("shard", "rep")),
    )
    out_specs = (
        P("role", ("shard", "rep"), None, None),
        P("role", "rep", "shard"),
        P("role", "rep", "shard"),
    )
    return jax.shard_map(body, mesh=mesh, in_specs=in_specs, out_specs=out_specs, check_vma=False)
```
